32 devices in a mesh: gx: 4 (over y, core), gy: 8 (over z, x).
Axes of the slice: x: 2, y: 2, z: 4, core: 2. Of those that a mesh axis runs over, the one named last changes fastest.
Arguments:
- source_field: float32 [2048, 16, 256], P('gx', 'gy'), may hold values from -6 to 6
- permeability: float32 [2048, 16, 256], P('gx', 'gy'), may hold values from 0.3 to 3
- layer_ids: int32 [256], replicated, may hold values from 0 to 3, as said below
- inverse_fine: float32 [4, 2048, 512], P(None, 'gx'), as said below
- couple_fine: float32 [2, 4, 4], P(None, None, 'gx'), may hold values from 0.35 to 0.7
- inverse_coarse: float32 [4, 2048, 512], P(None, 'gx'), as said below
- couple_coarse: float32 [2, 4, 4], P(None, None, 'gx'), may hold values from 0.35 to 0.7
- owner_map: int32 [8, 1], replicated, may hold values from 0 to 1
Outputs:
- solution_fine: float32 [2048, 16, 256], P('gx', 'gy')
- residual_fine: float32 [2048, 16, 256], P('gx', 'gy')
- solution_coarse: float32 [2048, 8, 256], P('gx', 'gy')
The draws below stay inside these ranges and needn't reach their ends.
Inputs may be any that keep to these rules, and one draw needn't show every extreme that they name: owner_map names the aggregate of each level-6 plane; every aggregate below 2 holds at least one plane. `layer_ids`: every rock type names the same number of z cells. `inverse_fine`: each block is a positive-definite dense matrix with a diagonal dominating each line solve's coupling. `inverse_coarse`: each block is a positive-definite dense matrix with a diagonal dominating each line solve's coupling.
All inputs are finite; a program needn't handle non-finite values.
Results may differ from the reference program's by a relative error of at most 0.00012.
Values sent between devices are 32-bit elements; how exact they have to be, the bound alone decides.
A program may use at most 128 MiB of HBM per device.

```python
import math
import jax
import jax.numpy as jnp
from jax import lax

CX = 512
NZ = 256
NL = 4
NSWEEP = 3
NX = 2048
NY5 = 16
NY6 = 8
NAGG = 2
N_GX = 4


def make_inverse(base_key):
    diag_key, noise_key = jax.random.split(base_key)
    row_index = jnp.arange(NX) % CX
    col_index = jnp.arange(CX)
    distance = jnp.abs(row_index[:, None] - col_index[None, :]).astype(jnp.float32)
    identity = (row_index[:, None] == col_index[None, :]).astype(jnp.float32)
    kernel = 0.5 * jnp.exp(-0.6 * distance / CX)
    diagonal = jax.random.uniform(diag_key, (NL, NX, 1), jnp.float32, 0.2, 0.5)
    noise_part = jax.random.uniform(noise_key, (NL, NX, CX), jnp.float32, -1.0, 1.0)
    noise_scale = 0.25 / math.sqrt(CX)
    return kernel[None] + identity[None] * diagonal + noise_scale * noise_part


def draw_inverse_fine(key, part):
    return make_inverse(jax.random.fold_in(key, 11))


def draw_inverse_coarse(key, part):
    return make_inverse(jax.random.fold_in(key, 23))


def draw_layer_ids(key, part):
    shuffled = jax.random.permutation(jax.random.fold_in(key, 37), NZ)
    return (shuffled % NL).astype(jnp.int32)


def block_levels(own_key, shape, shards, least, high):
    gain, own = 1.0, jax.random.fold_in(own_key, 6)
    for axis_at, blocks in shards:
        steps = jnp.exp(jax.random.uniform(jax.random.fold_in(own, axis_at), (blocks,), jnp.float32, least / len(shards), high / len(shards)))
        gain = gain * jnp.repeat(steps, shape[axis_at] // blocks).reshape([-1 if axis == axis_at else 1 for axis in range(len(shape))])
    return gain


def picks_of(stream_key, rows, number_of, top, lift):
    sequence = jax.random.permutation(jax.random.fold_in(stream_key, 1), number_of)
    pull = sequence
    for power in range(3):
        pull = pull * pull // number_of
    pull = pull * lift // number_of
    chance = jax.random.randint(jax.random.fold_in(stream_key, 2), (rows, number_of), 0, 4096) + pull
    sure = jax.random.permutation(jax.random.fold_in(stream_key, 3), rows)[jnp.arange(number_of) % rows]
    chance = jnp.where(jnp.arange(rows)[:, None] == sure[None, :], 1 << 14, chance)
    score = chance * number_of + jnp.arange(number_of)
    return lax.top_k(score.astype(jnp.int32), top)[1].astype(jnp.int32)


def bell_draw(own_key, dims, width, bound, cuts=(), kind=jnp.bfloat16):
    values = width * jax.random.normal(own_key, dims, jnp.float32)
    if cuts:
        values = values * block_levels(own_key, dims, cuts, -0.22, 0.18)
    return jnp.clip(values, -bound, bound).astype(kind)


def setup_inputs(seed: int = 0) -> dict:
    arg_keys = jax.random.split(jax.random.key(seed), 9)
    return {
        "source_field": bell_draw(arg_keys[0], (NX, NY5, NZ), 1.0, 6.0, ((0, 4), (1, 8)), jnp.float32),
        "permeability": jnp.clip(jnp.exp(math.log(3.0) - 2.3025851 * jax.random.uniform(arg_keys[1], (NX, NY5, NZ), jnp.float32) ** block_levels(arg_keys[1], (NX, NY5, NZ), ((0, 4), (1, 8)), -0.2, 0.2)), 0.3, 3.0),
        "layer_ids": draw_layer_ids(jax.random.fold_in(arg_keys[8], 71), 0),
        "inverse_fine": draw_inverse_fine(jax.random.fold_in(arg_keys[8], 71), 0),
        "couple_fine": jnp.clip(0.35 + 0.35 * jax.random.uniform(arg_keys[4], (2, NL, N_GX), jnp.float32) ** block_levels(arg_keys[4], (2, NL, N_GX), ((2, 4),), -0.2, 0.2), 0.35, 0.7),
        "inverse_coarse": draw_inverse_coarse(jax.random.fold_in(arg_keys[8], 71), 0),
        "couple_coarse": jnp.clip(0.35 + 0.35 * jax.random.uniform(arg_keys[6], (2, NL, N_GX), jnp.float32) ** block_levels(arg_keys[6], (2, NL, N_GX), ((2, 4),), -0.2, 0.2), 0.35, 0.7),
        "owner_map": picks_of(arg_keys[7], NY6, NAGG, 1, 4096),
    }


PRECISE = lax.Precision.HIGHEST
WEIGHTS = (0.5, 0.5, 0.15, 0.15, 0.05, 0.05)
STORAGE = 0.1


def neighbours(padded):
    return [padded[:-2, 1:-1, 1:-1], padded[2:, 1:-1, 1:-1], padded[1:-1, :-2, 1:-1],
            padded[1:-1, 2:, 1:-1], padded[1:-1, 1:-1, :-2], padded[1:-1, 1:-1, 2:]]


def face_terms(padded):
    centre = padded[1:-1, 1:-1, 1:-1]
    return [weight * 2.0 * centre * beside / (centre + beside) for weight, beside in zip(WEIGHTS, neighbours(padded))]


def apply_operator(padded, face_list):
    centre = padded[1:-1, 1:-1, 1:-1]
    result_sum = STORAGE * centre
    for face_term, beside in zip(face_list, neighbours(padded)):
        result_sum = result_sum + face_term * (centre - beside)
    return result_sum


def chain_solve(chain_rows):
    blocks_count = chain_rows.shape[0]
    carry_value = jnp.zeros_like(chain_rows[0, 0])
    carry_gain = jnp.zeros_like(chain_rows[0, 0])
    first_parts, first_links, last_parts, last_links = [], [], [], []
    for block_index in range(blocks_count):
        pivot_value = 1.0 - chain_rows[block_index, 2] * carry_gain
        first_part = (chain_rows[block_index, 0] - chain_rows[block_index, 2] * carry_value) / pivot_value
        first_link = chain_rows[block_index, 4] / pivot_value
        carry_value = chain_rows[block_index, 1] - chain_rows[block_index, 3] * carry_value + chain_rows[block_index, 3] * carry_gain * first_part
        carry_gain = chain_rows[block_index, 5] + chain_rows[block_index, 3] * carry_gain * first_link
        first_parts.append(first_part)
        first_links.append(first_link)
        last_parts.append(carry_value)
        last_links.append(carry_gain)
    following = jnp.zeros_like(carry_value)
    last_values = [following] * blocks_count
    next_values = [following] * blocks_count
    for block_index in range(blocks_count - 1, -1, -1):
        next_values[block_index] = following
        last_values[block_index] = last_parts[block_index] - last_links[block_index] * following
        following = first_parts[block_index] - first_links[block_index] * following
    previous = [jnp.zeros_like(following)] + last_values[:-1]
    return jnp.stack([jnp.stack([previous[block_index], next_values[block_index]]) for block_index in range(blocks_count)])


def line_solve(source, inverse, couple, layer_ids):
    blocks_count = couple.shape[2]
    block_width = inverse.shape[2]
    line_count = source.shape[1]
    blocks = inverse.reshape(inverse.shape[0], blocks_count, block_width, block_width)

    def per_depth(depth_index):
        layer_index = layer_ids[depth_index]
        matrix = blocks[layer_index]
        lower_couple = couple[0, layer_index]
        upper_couple = couple[1, layer_index]
        column = lax.dynamic_index_in_dim(source, depth_index, 2, keepdims=False).reshape(blocks_count, block_width, line_count)
        values = jnp.einsum("pic,pcy->piy", matrix, column, precision=PRECISE)
        shaped = (blocks_count, line_count)
        chain_rows = jnp.stack([
            values[:, 0, :], values[:, -1, :],
            jnp.broadcast_to((lower_couple * matrix[:, 0, 0])[:, None], shaped),
            jnp.broadcast_to((lower_couple * matrix[:, -1, 0])[:, None], shaped),
            jnp.broadcast_to((upper_couple * matrix[:, 0, -1])[:, None], shaped),
            jnp.broadcast_to((upper_couple * matrix[:, -1, -1])[:, None], shaped)], axis=1)
        solved = chain_solve(chain_rows)
        result = values - (lower_couple[:, None] * solved[:, 0, :])[:, None, :] * matrix[:, :, 0][:, :, None] \
            - (upper_couple[:, None] * solved[:, 1, :])[:, None, :] * matrix[:, :, -1][:, :, None]
        return result.reshape(blocks_count * block_width, line_count)

    depths = jnp.arange(source.shape[2], dtype=jnp.int32)
    return jnp.transpose(lax.map(per_depth, depths), (1, 2, 0))


def reference(source_field, permeability, layer_ids, inverse_fine, couple_fine, inverse_coarse, couple_coarse, owner_map):
    face_list = face_terms(jnp.pad(permeability, 1))
    solution = jnp.zeros_like(source_field)
    for sweep_index in range(NSWEEP):
        update = source_field - apply_operator(jnp.pad(solution, 1), face_list)
        solution = solution + line_solve(update, inverse_fine, couple_fine, layer_ids)
    residual = source_field - apply_operator(jnp.pad(solution, 1), face_list)
    coarse = 0.5 * (residual[:, 0::2, :] + residual[:, 1::2, :])
    owners = owner_map[:, 0]
    member = (owners[:, None] == jnp.arange(NAGG, dtype=jnp.int32)[None, :]).astype(jnp.float32)
    aggregate = jnp.einsum("xjz,jo->xoz", coarse, member, precision=PRECISE)
    smoothed = line_solve(aggregate, inverse_coarse, couple_coarse, layer_ids)
    solution_coarse = jnp.take(smoothed, owners, axis=1)
    return solution, residual, solution_coarse
```

```python
import jax
import jax.numpy as jnp
from jax import lax
from jax.sharding import PartitionSpec as P

NSWEEP = 3
WEIGHTS = (0.5, 0.15, 0.05)
STORAGE = 0.1
F32 = jnp.float32


def shift_from(array, axis, step):
    peers = lax.axis_size(axis)
    pairs = [(i, i + step) for i in range(peers) if 0 <= i + step < peers]
    return lax.ppermute(array, axis, pairs)


def face(weight, one, two):
    return weight * 2.0 * one * two / (one + two)


def gains(rows):
    gain = jnp.zeros_like(rows[0, 0])
    out = []
    for p in range(rows.shape[0]):
        inv = 1.0 / (1.0 - rows[p, 0] * gain)
        link = rows[p, 2] * inv
        back = rows[p, 1] * gain
        gain = rows[p, 3] + back * link
        out.append((rows[p, 0], rows[p, 1], inv, link, back, gain))
    return out


def chain(values, parts):
    count = len(parts)
    carry = jnp.zeros_like(values[0, 0])
    firsts, lasts = [], []
    for p, (low_first, low_last, inv, link, back, gain) in enumerate(parts):
        first = (values[p, 0] - low_first * carry) * inv
        carry = values[p, 1] - low_last * carry + back * first
        firsts.append(first)
        lasts.append(carry)
    following = jnp.zeros_like(carry)
    ends, nexts = [None] * count, [None] * count
    for p in range(count - 1, -1, -1):
        nexts[p] = following
        ends[p] = lasts[p] - parts[p][5] * following
        following = firsts[p] - parts[p][3] * following
    previous = [jnp.zeros_like(following)] + ends[:-1]
    return jnp.stack([jnp.stack([a, b]) for a, b in zip(previous, nexts)])


def local(source, perm, layer_ids, inv_fine, cpl_fine, inv_coarse, cpl_coarse, owner_map):
    width, planes, depth = source.shape
    layers = inv_fine.shape[0]
    gx = lax.axis_index("gx")
    src = jnp.transpose(source, (1, 0, 2))
    k = jnp.transpose(perm, (1, 0, 2))
    up = shift_from(jnp.stack([src[-1], k[-1]]), "gy", 1)
    down = shift_from(jnp.stack([src[0], k[0]]), "gy", -1)
    kx_before = shift_from(k[:, -1:], "gx", 1)
    kx_after = shift_from(k[:, :1], "gx", -1)
    masks = [layer_ids == i for i in range(layers)]

    def pick(per_layer):
        out = jnp.zeros(per_layer.shape[1:] + (depth,), F32)
        for i in range(layers):
            out = jnp.where(masks[i], per_layer[i][..., None], out)
        return out

    def couplings(matrix, couple):
        low, high = couple[0, :, 0], couple[1, :, 0]
        return jnp.stack([low * matrix[:, 0, 0], low * matrix[:, -1, 0], high * matrix[:, 0, -1], high * matrix[:, -1, -1]], 1)

    both = jnp.concatenate([couplings(inv_fine, cpl_fine), couplings(inv_coarse, cpl_coarse)], 1)
    every = lax.all_gather(both, "gx")
    every = jnp.stack([pick(every[p]) for p in range(every.shape[0])])
    parts_fine, parts_coarse = gains(every[:, :4]), gains(every[:, 4:])

    def edges(matrix, couple):
        return pick(couple[0] * matrix[:, :, 0]), pick(couple[1] * matrix[:, :, -1])

    edges_fine, edges_coarse = edges(inv_fine, cpl_fine), edges(inv_coarse, cpl_coarse)

    def solve(field, matrix, parts, columns):
        flat = jnp.transpose(field, (1, 0, 2)).reshape(width, -1)
        mask_all = [jnp.tile(m, field.shape[0]) for m in masks]
        value = None
        for i in range(layers):
            v = jnp.dot(matrix[i], flat, precision=lax.Precision.HIGH)
            value = v if value is None else jnp.where(mask_all[i], v, value)
        value = jnp.transpose(value.reshape(width, -1, depth), (1, 0, 2))
        ends = lax.all_gather(jnp.stack([value[:, 0], value[:, -1]]), "gx")
        solved = lax.dynamic_index_in_dim(chain(ends, parts), gx, 0, keepdims=False)
        return value - solved[0][:, None] * columns[0] - solved[1][:, None] * columns[1], solved

    kx = jnp.concatenate([kx_before, k, kx_after], 1)
    fx = face(WEIGHTS[0], kx[:, :-1], kx[:, 1:])
    ky = jnp.concatenate([up[1][None], k, down[1][None]], 0)
    fy = face(WEIGHTS[1], ky[:-1], ky[1:])
    kz = jnp.pad(k, ((0, 0), (0, 0), (1, 1)))
    fz = face(WEIGHTS[2], kz[:, :, :-1], kz[:, :, 1:])

    def residual_of(u, u_before, u_after, u_up, u_down):
        ux = jnp.concatenate([u_before[:, None], u, u_after[:, None]], 1)
        uy = jnp.concatenate([u_up[None], u, u_down[None]], 0)
        uz = jnp.pad(u, ((0, 0), (0, 0), (1, 1)))
        dx = fx * (ux[:, 1:] - ux[:, :-1])
        dy = fy * (uy[1:] - uy[:-1])
        dz = fz * (uz[:, :, 1:] - uz[:, :, :-1])
        flow = dx[:, :-1] - dx[:, 1:] + dy[:-1] - dy[1:] + dz[:, :, :-1] - dz[:, :, 1:]
        return src - (STORAGE * u + flow)

    first = jnp.concatenate([src, up[:1], down[:1]], 0)
    u, ends = solve(first, inv_fine, parts_fine, edges_fine)
    u, u_up, u_down = u[:planes], u[planes], u[planes + 1]
    ends = ends[:, :planes]
    residual = residual_of(u, ends[0], ends[1], u_up, u_down)
    for _ in range(NSWEEP - 1):
        change, more = solve(residual, inv_fine, parts_fine, edges_fine)
        u = u + change
        ends = ends + more
        u_up = shift_from(u[-1], "gy", 1)
        u_down = shift_from(u[0], "gy", -1)
        residual = residual_of(u, ends[0], ends[1], u_up, u_down)
    coarse = 0.5 * (residual[0] + residual[1])
    smooth, _ = solve(coarse[None], inv_coarse, parts_coarse, edges_coarse)
    groups = lax.axis_size("gy")
    owners = owner_map[:, 0]
    chunks = smooth[0].reshape(groups, width // groups, depth)
    here = lax.all_to_all(chunks, "gy", 0, 0)
    same = (owners[:, None] == owners[None, :]).astype(F32)
    summed = sum(same[:, j, None, None] * here[j][None] for j in range(groups))
    result = lax.all_to_all(summed, "gy", 0, 0).reshape(width, 1, depth)
    return jnp.transpose(u, (1, 0, 2)), jnp.transpose(residual, (1, 0, 2)), result


def solution(mesh):
    in_specs = (
        P("gx", "gy", None),
        P("gx", "gy", None),
        P(),
        P(None, "gx", None),
        P(None, None, "gx"),
        P(None, "gx", None),
        P(None, None, "gx"),
        P(),
    )
    out_specs = (P("gx", "gy", None), P("gx", "gy", None), P("gx", "gy", None))
    return jax.shard_map(local, mesh=mesh, in_specs=in_specs, out_specs=out_specs, check_vma=False)
```

```python
import functools
import jax
import jax.numpy as jnp
from jax import lax
from jax.experimental import pallas as pl
from jax.experimental.pallas import tpu as pltpu
from jax.sharding import PartitionSpec as P

NSWEEP = 3
WEIGHTS = (0.5, 0.15, 0.05)
STORAGE = 0.1
F32 = jnp.float32
BF16 = jnp.bfloat16
MESH = pl.DeviceIdType.MESH


def face(weight, one, two):
    return weight * 2.0 * one * two / (one + two)


def gains(rows):
    gain = jnp.zeros_like(rows[0][0])
    out = []
    for low_first, low_last, high_first, high_last in rows:
        inv = 1.0 / (1.0 - low_first * gain)
        link = high_first * inv
        back = low_last * gain
        gain = high_last + back * link
        out.append((low_first, low_last, inv, link, back, gain))
    return out


def chain(values, parts, own):
    count = len(parts)
    carry = jnp.zeros_like(values[0][0])
    firsts, lasts = [], []
    for (head, tail), (low_first, low_last, inv, link, back, gain) in zip(values, parts):
        first = (head - low_first * carry) * inv
        carry = tail - low_last * carry + back * first
        firsts.append(first)
        lasts.append(carry)
    following = jnp.zeros_like(carry)
    previous, after = following, following
    for p in range(count - 1, -1, -1):
        after = jnp.where(own == p, following, after)
        end = lasts[p] - parts[p][5] * following
        previous = jnp.where(own == p + 1, end, previous)
        following = firsts[p] - parts[p][3] * following
    return previous, after


def kernel(n, m, src, k, inv_f, inv_c, edge, coef, ids, same, u_out, r_out, c_out,
           hi, lo, g_hi, g_lo, val, halo, u_s, u_h, r_s, txb, txa, tzb, tza, ty,
           coefs, vals, sm, got, mix, back, h_send, h_recv, g_send, g_recv, a_send, a_recv):
    gx, gy = lax.axis_index("gx"), lax.axis_index("gy")
    width, depth = val.shape[1:]
    layers = hi.shape[0]
    planes = [slice(0, depth), slice(depth, 2 * depth)]
    row = lax.broadcasted_iota(jnp.int32, (width, depth), 0)
    lane = lax.broadcasted_iota(jnp.int32, (width, depth), 1)

    def halo_copy(kind, way, source):
        peer = gy + 1 if way == 0 else gy - 1
        return pltpu.make_async_remote_copy(
            src_ref=source, dst_ref=halo.at[kind, way],
            send_sem=h_send.at[kind, way], recv_sem=h_recv.at[kind, way],
            device_id={"gy": peer}, device_id_type=MESH)

    def can_send(way):
        return gy < m - 1 if way == 0 else gy > 0

    def comes(way):
        return gy > 0 if way == 0 else gy < m - 1

    def send_halo(kind, way, source):
        @pl.when(can_send(way))
        def _():
            halo_copy(kind, way, source).start()

    def wait_halo(kind, way, source):
        @pl.when(comes(way))
        def _():
            halo_copy(kind, way, source).wait_recv()

    def sent_halo(kind, way, source):
        @pl.when(can_send(way))
        def _():
            halo_copy(kind, way, source).wait_send()

    def gather(i, ref):
        out = []
        for d in range(1, n):
            out.append(pltpu.make_async_remote_copy(
                src_ref=ref.at[gx + 1], dst_ref=ref.at[gx + 1],
                send_sem=g_send.at[i, d - 1], recv_sem=g_recv.at[i, d - 1],
                device_id={"gx": lax.rem(gx + d, n)}, device_id_type=MESH))
        return out

    barrier = pltpu.get_barrier_semaphore()
    for d in range(1, n):
        pl.semaphore_signal(barrier, inc=1, device_id={"gx": lax.rem(gx + d, n)}, device_id_type=MESH)
    for d in range(1, m):
        pl.semaphore_signal(barrier, inc=1, device_id={"gy": lax.rem(gy + d, m)}, device_id_type=MESH)

    zero_rows = jnp.zeros(coefs.shape[1:], F32)
    coefs[0] = zero_rows
    coefs[n + 1] = zero_rows
    coefs[gx + 1, 0:8] = coef[...]
    for y in range(2):
        coefs[gx + 1, 8 + y : 9 + y] = k[0:1, planes[y]]
        coefs[gx + 1, 10 + y : 11 + y] = k[width - 1 : width, planes[y]]
    for way in range(2):
        @pl.when(jnp.logical_not(comes(way)))
        def _():
            for kind in range(4):
                halo[kind, way] = jnp.zeros((width, depth), F32)

    pl.semaphore_wait(barrier, n + m - 2)
    ends_of = [planes[1], planes[0]]
    for kind, ref in ((0, src), (1, k)):
        for way in range(2):
            send_halo(kind, way, ref.at[:, ends_of[way]])
    first_gather = gather(0, coefs)
    for c in first_gather:
        c.start()

    def split_matrices(ref):
        def body(i, _):
            b = ref[i]
            h = b.astype(BF16)
            hi[i] = h
            lo[i] = (b - h.astype(F32)).astype(BF16)
            return 0
        lax.fori_loop(0, layers, body, 0)

    def multiply(field, slot):
        h = field.astype(BF16)
        g_hi[...] = h
        g_lo[...] = (field - h.astype(F32)).astype(BF16)

        def body(i, _):
            v = jnp.dot(hi[i], g_hi[...], preferred_element_type=F32)
            v = v + jnp.dot(hi[i], g_lo[...], preferred_element_type=F32)
            v = v + jnp.dot(lo[i], g_hi[...], preferred_element_type=F32)
            val[slot] = jnp.where(ids[...] == i, v, val[slot])
            return 0

        val[slot] = jnp.zeros((width, depth), F32)
        lax.fori_loop(0, layers, body, 0)

    def solve_ends(i, slots, parts):
        for s in slots:
            vals[i, gx + 1, s : s + 1] = val[s, 0:1]
            vals[i, gx + 1, 4 + s : 5 + s] = val[s, width - 1 : width]
        copies = gather(1 + i, vals.at[i])
        for c in copies:
            c.start()
        for c in copies:
            c.wait_recv()
        count = len(slots)
        values = [(vals[i, p + 1, 0:count], vals[i, p + 1, 4 : 4 + count]) for p in range(n)]
        previous, after = chain(values, parts, gx)
        return previous, after, copies

    def edge_columns(base):
        out = []
        for side in range(2):
            at = base + side * layers
            total = jnp.zeros((width, depth), F32)
            for i in range(layers):
                total = jnp.where(ids[...] == i, edge[:, at + i : at + i + 1], total)
            out.append(total)
        return out

    def corrected(s, previous, after, base):
        low, high = edge_columns(base)
        return val[s] - previous[s : s + 1] * low - after[s : s + 1] * high

    split_matrices(inv_f)
    for y in range(2):
        multiply(src[:, planes[y]], y)
    for c in first_gather:
        c.wait_recv()
    every = [[coefs[p + 1, i : i + 1] for i in range(8)] for p in range(n)]
    parts_fine = gains([e[:4] for e in every])
    parts_coarse = gains([e[4:] for e in every])

    for y in range(2):
        kc = k[:, planes[y]]
        before = jnp.where(row == 0, coefs[gx, 10 + y : 11 + y], pltpu.roll(kc, 1, 0))
        after = jnp.where(row == width - 1, coefs[gx + 2, 8 + y : 9 + y], pltpu.roll(kc, width - 1, 0))
        txb[y] = face(WEIGHTS[0], kc, before)
        txa[y] = face(WEIGHTS[0], kc, after)
        tzb[y] = jnp.where(lane == 0, 0.0, face(WEIGHTS[2], kc, pltpu.roll(kc, 1, 1)))
        tza[y] = jnp.where(lane == depth - 1, 0.0, face(WEIGHTS[2], kc, pltpu.roll(kc, depth - 1, 1)))
    ty[1] = face(WEIGHTS[1], k[:, planes[0]], k[:, planes[1]])

    for way in range(2):
        wait_halo(0, way, src.at[:, ends_of[way]])
        multiply(halo[0, way], 2 + way)
    previous, after, sent0 = solve_ends(0, [0, 1, 2, 3], parts_fine)
    for y in range(2):
        u_s[0, y] = corrected(y, previous, after, 0)
    for way in range(2):
        u_h[way] = corrected(2 + way, previous, after, 0)
    sums = [previous[0:2], after[0:2]]
    all_sent = [first_gather, sent0]

    for way in range(2):
        wait_halo(1, way, k.at[:, ends_of[way]])
        ty[2 * way] = face(WEIGHTS[1], halo[1, way], k[:, planes[way]])

    def inner_residual(t, y):
        u = u_s[t, y]
        before = jnp.where(row == 0, sums[0][y : y + 1], pltpu.roll(u, 1, 0))
        after = jnp.where(row == width - 1, sums[1][y : y + 1], pltpu.roll(u, width - 1, 0))
        total = STORAGE * u + txb[y] * (u - before) + txa[y] * (u - after)
        total = total + ty[1] * (u - u_s[t, 1 - y])
        total = total + tzb[y] * (u - pltpu.roll(u, 1, 1)) + tza[y] * (u - pltpu.roll(u, depth - 1, 1))
        r_s[y] = src[:, planes[y]] - total

    def outer_residual(t, y, beside):
        return r_s[y] - ty[2 * y] * (u_s[t, y] - beside)

    for t in range(1, NSWEEP):
        for y in range(2):
            inner_residual(t - 1, y)
        for y in range(2):
            if t == 1:
                beside = u_h[y]
            else:
                wait_halo(t, y, u_s.at[t - 1, 1 - y])
                beside = halo[t, y]
            multiply(outer_residual(t - 1, y, beside), y)
        previous, after, more = solve_ends(t, [0, 1], parts_fine)
        all_sent.append(more)
        sums = [sums[0] + previous, sums[1] + after]
        for way in range(2):
            y = 1 - way
            u_s[t, y] = u_s[t - 1, y] + corrected(y, previous, after, 0)
            send_halo(t + 1, way, u_s.at[t, y])
    split_matrices(inv_c)
    for y in range(2):
        inner_residual(NSWEEP - 1, y)
        u_out[:, planes[y]] = u_s[NSWEEP - 1, y]
    coarse = None
    for y in range(2):
        wait_halo(NSWEEP, y, u_s.at[NSWEEP - 1, 1 - y])
        r = outer_residual(NSWEEP - 1, y, halo[NSWEEP, y])
        r_out[:, planes[y]] = r
        coarse = r if coarse is None else 0.5 * (coarse + r)
    multiply(coarse, 0)
    previous, after, more = solve_ends(NSWEEP, [0], parts_coarse)
    all_sent.append(more)
    sm[...] = corrected(0, previous, after, 2 * layers).reshape(sm.shape)

    def exchange(i, source, target):
        out = []
        for d in range(1, m):
            peer = lax.rem(gy + d, m)
            out.append(pltpu.make_async_remote_copy(
                src_ref=source.at[peer], dst_ref=target.at[gy],
                send_sem=a_send.at[i, d - 1], recv_sem=a_recv.at[i, d - 1],
                device_id={"gy": peer}, device_id_type=MESH))
        for c in out:
            c.start()
        target[gy] = source[gy]
        for c in out:
            c.wait_recv()
        return out

    all_sent.append(exchange(0, sm, got))

    def mix_rows(j, _):
        def add(i, total):
            return total + same[j, i] * got[i]
        mix[j] = lax.fori_loop(0, m, add, jnp.zeros(got.shape[1:], F32))
        return 0

    lax.fori_loop(0, m, mix_rows, 0)
    all_sent.append(exchange(1, mix, back))
    c_out[...] = back[...]
    for copies in all_sent:
        for c in copies:
            c.wait_send()
    for kind, ref in ((0, src), (1, k)):
        for way in range(2):
            sent_halo(kind, way, ref.at[:, ends_of[way]])
    for t in range(1, NSWEEP):
        for way in range(2):
            sent_halo(t + 1, way, u_s.at[t, 1 - way])


def local(source, perm, layer_ids, inv_fine, cpl_fine, inv_coarse, cpl_coarse, owner_map):
    width, planes, depth = source.shape
    layers = inv_fine.shape[0]
    n, m = lax.axis_size("gx"), lax.axis_size("gy")

    def columns(matrix, couple):
        return [couple[0] * matrix[:, :, 0], couple[1] * matrix[:, :, -1]]

    sides = columns(inv_fine, cpl_fine) + columns(inv_coarse, cpl_coarse)
    edge = jnp.transpose(jnp.concatenate(sides, 0))
    rows = jnp.stack([s[:, at] for s in sides for at in (0, -1)])
    coef = jnp.zeros((rows.shape[0], depth), F32)
    for i in range(layers):
        coef = jnp.where(layer_ids == i, rows[:, i : i + 1], coef)
    owners = owner_map[:, 0]
    same = (owners[:, None] == owners[None, :]).astype(F32)
    chunk = (m, width // m, depth)
    plane = (width, depth)
    flat = (width, planes * depth)
    vmem = pl.BlockSpec(memory_space=pltpu.VMEM)
    u, r, c = pl.pallas_call(
        functools.partial(kernel, n, m),
        out_shape=[jax.ShapeDtypeStruct(flat, F32), jax.ShapeDtypeStruct(flat, F32), jax.ShapeDtypeStruct(chunk, F32)],
        in_specs=[vmem] * 7 + [pl.BlockSpec(memory_space=pltpu.SMEM)],
        out_specs=[vmem] * 3,
        scratch_shapes=[
            pltpu.VMEM(inv_fine.shape, BF16),
            pltpu.VMEM(inv_fine.shape, BF16),
            pltpu.VMEM(plane, BF16),
            pltpu.VMEM(plane, BF16),
            pltpu.VMEM((4,) + plane, F32),
            pltpu.VMEM((4, 2) + plane, F32),
            pltpu.VMEM((NSWEEP, 2) + plane, F32),
            pltpu.VMEM((2,) + plane, F32),
            pltpu.VMEM((2,) + plane, F32),
            pltpu.VMEM((2,) + plane, F32),
            pltpu.VMEM((2,) + plane, F32),
            pltpu.VMEM((2,) + plane, F32),
            pltpu.VMEM((2,) + plane, F32),
            pltpu.VMEM((3,) + plane, F32),
            pltpu.VMEM((n + 2, 16, depth), F32),
            pltpu.VMEM((NSWEEP + 1, n + 2, 8, depth), F32),
            pltpu.VMEM(chunk, F32),
            pltpu.VMEM(chunk, F32),
            pltpu.VMEM(chunk, F32),
            pltpu.VMEM(chunk, F32),
            pltpu.SemaphoreType.DMA((4, 2)),
            pltpu.SemaphoreType.DMA((4, 2)),
            pltpu.SemaphoreType.DMA((NSWEEP + 2, n - 1)),
            pltpu.SemaphoreType.DMA((NSWEEP + 2, n - 1)),
            pltpu.SemaphoreType.DMA((2, m - 1)),
            pltpu.SemaphoreType.DMA((2, m - 1)),
        ],
        compiler_params=pltpu.CompilerParams(collective_id=0, has_side_effects=True, vmem_limit_bytes=56 << 20),
    )(source.reshape(flat), perm.reshape(flat), inv_fine, inv_coarse, edge, coef, layer_ids[None], same)
    return u.reshape(source.shape), r.reshape(source.shape), c.reshape(width, 1, depth)


def solution(mesh):
    in_specs = (
        P("gx", "gy", None),
        P("gx", "gy", None),
        P(),
        P(None, "gx", None),
        P(None, None, "gx"),
        P(None, "gx", None),
        P(None, None, "gx"),
        P(),
    )
    out_specs = (P("gx", "gy", None), P("gx", "gy", None), P("gx", "gy", None))
    return jax.shard_map(local, mesh=mesh, in_specs=in_specs, out_specs=out_specs, check_vma=False)
```

```python
import functools
import jax
import jax.numpy as jnp
from jax import lax
from jax.experimental import pallas as pl
from jax.experimental.pallas import tpu as pltpu
from jax.sharding import PartitionSpec as P

NSWEEP = 3
WEIGHTS = (0.5, 0.15, 0.05)
STORAGE = 0.1
F32 = jnp.float32
BF16 = jnp.bfloat16
MESH = pl.DeviceIdType.MESH


def face(weight, one, two):
    return weight * 2.0 * one * two / (one + two)


def gains(rows):
    gain = jnp.zeros_like(rows[0][0])
    out = []
    for low_first, low_last, high_first, high_last in rows:
        inv = 1.0 / (1.0 - low_first * gain)
        link = high_first * inv
        back = low_last * gain
        gain = high_last + back * link
        out.append((low_first, low_last, inv, link, back, gain))
    return out


def chain(values, parts, own):
    count = len(parts)
    carry = jnp.zeros_like(values[0][0])
    firsts, lasts = [], []
    for (head, tail), (low_first, low_last, inv, link, back, gain) in zip(values, parts):
        first = (head - low_first * carry) * inv
        carry = tail - low_last * carry + back * first
        firsts.append(first)
        lasts.append(carry)
    following = jnp.zeros_like(carry)
    previous, after = following, following
    for p in range(count - 1, -1, -1):
        after = jnp.where(own == p, following, after)
        end = lasts[p] - parts[p][5] * following
        previous = jnp.where(own == p + 1, end, previous)
        following = firsts[p] - parts[p][3] * following
    return previous, after


def kernel(n, m, src, k, inv_f, inv_c, ids, cpl_f, cpl_c, same, u_out, r_out, c_out,
           hi, lo, g_hi, g_lo, val, halo, u_s, u_h, r_s, txb, txa, tzb, tza, ty,
           coefs, vals, sm, got, mix, back, cols, h_send, h_recv, g_send, g_recv, a_send, a_recv):
    gx, gy = lax.axis_index("gx"), lax.axis_index("gy")
    width, depth = val.shape[1:]
    layers = hi.shape[0]
    planes = [slice(0, depth), slice(depth, 2 * depth)]
    row = lax.broadcasted_iota(jnp.int32, (width, depth), 0)
    lane = lax.broadcasted_iota(jnp.int32, (width, depth), 1)

    def halo_copy(kind, way, source):
        peer = gy + 1 if way == 0 else gy - 1
        return pltpu.make_async_remote_copy(
            src_ref=source, dst_ref=halo.at[kind, way],
            send_sem=h_send.at[kind, way], recv_sem=h_recv.at[kind, way],
            device_id={"gy": peer}, device_id_type=MESH)

    def can_send(way):
        return gy < m - 1 if way == 0 else gy > 0

    def comes(way):
        return gy > 0 if way == 0 else gy < m - 1

    def send_halo(kind, way, source):
        @pl.when(can_send(way))
        def _():
            halo_copy(kind, way, source).start()

    def wait_halo(kind, way, source):
        @pl.when(comes(way))
        def _():
            halo_copy(kind, way, source).wait_recv()

    def sent_halo(kind, way, source):
        @pl.when(can_send(way))
        def _():
            halo_copy(kind, way, source).wait_send()

    def gather(i, ref):
        out = []
        for d in range(1, n):
            out.append(pltpu.make_async_remote_copy(
                src_ref=ref.at[gx + 1], dst_ref=ref.at[gx + 1],
                send_sem=g_send.at[i, d - 1], recv_sem=g_recv.at[i, d - 1],
                device_id={"gx": lax.rem(gx + d, n)}, device_id_type=MESH))
        return out

    barrier = pltpu.get_barrier_semaphore()
    for d in range(1, n):
        pl.semaphore_signal(barrier, inc=1, device_id={"gx": lax.rem(gx + d, n)}, device_id_type=MESH)
    for d in range(1, m):
        pl.semaphore_signal(barrier, inc=1, device_id={"gy": lax.rem(gy + d, m)}, device_id_type=MESH)

    zero_rows = jnp.zeros(coefs.shape[1:], F32)
    coefs[0] = zero_rows
    coefs[n + 1] = zero_rows
    for y in range(2):
        coefs[gx + 1, 8 + y : 9 + y] = k[0:1, planes[y]]
        coefs[gx + 1, 10 + y : 11 + y] = k[width - 1 : width, planes[y]]
    for way in range(2):
        @pl.when(jnp.logical_not(comes(way)))
        def _():
            for kind in range(4):
                halo[kind, way] = jnp.zeros((width, depth), F32)

    pl.semaphore_wait(barrier, n + m - 2)
    ends_of = [planes[1], planes[0]]
    for kind, ref in ((0, src), (1, k)):
        for way in range(2):
            send_halo(kind, way, ref.at[:, ends_of[way]])
    for side in range(2):
        at = (width - 1) * side
        for base, inv, cpl in ((0, inv_f, cpl_f), (2, inv_c, cpl_c)):
            total = jnp.zeros((width, depth), F32)
            for i in range(layers):
                total = jnp.where(ids[...] == i, cpl[side, i, 0] * inv[i, :, at : at + 1], total)
            cols[base + side] = total
    for i in range(4):
        coefs[gx + 1, 2 * i : 2 * i + 1] = cols[i, 0:1]
        coefs[gx + 1, 2 * i + 1 : 2 * i + 2] = cols[i, width - 1 : width]
    first_gather = gather(0, coefs)
    for c in first_gather:
        c.start()

    def split_matrices(ref):
        def body(i, _):
            b = ref[i]
            h = b.astype(BF16)
            hi[i] = h
            lo[i] = (b - h.astype(F32)).astype(BF16)
            return 0
        lax.fori_loop(0, layers, body, 0)

    def multiply(field, slot):
        h = field.astype(BF16)
        g_hi[...] = h
        g_lo[...] = (field - h.astype(F32)).astype(BF16)

        def body(i, _):
            v = jnp.dot(hi[i], g_hi[...], preferred_element_type=F32)
            v = v + jnp.dot(hi[i], g_lo[...], preferred_element_type=F32)
            v = v + jnp.dot(lo[i], g_hi[...], preferred_element_type=F32)
            val[slot] = jnp.where(ids[...] == i, v, val[slot])
            return 0

        val[slot] = jnp.zeros((width, depth), F32)
        lax.fori_loop(0, layers, body, 0)

    def solve_ends(i, slots, parts):
        for s in slots:
            vals[i, gx + 1, s : s + 1] = val[s, 0:1]
            vals[i, gx + 1, 4 + s : 5 + s] = val[s, width - 1 : width]
        copies = gather(1 + i, vals.at[i])
        for c in copies:
            c.start()
        for c in copies:
            c.wait_recv()
        count = len(slots)
        values = [(vals[i, p + 1, 0:count], vals[i, p + 1, 4 : 4 + count]) for p in range(n)]
        previous, after = chain(values, parts, gx)
        return previous, after, copies

    def corrected(s, previous, after, base):
        return val[s] - previous[s : s + 1] * cols[base] - after[s : s + 1] * cols[base + 1]

    split_matrices(inv_f)
    for y in range(2):
        multiply(src[:, planes[y]], y)
    for c in first_gather:
        c.wait_recv()
    every = [[coefs[p + 1, i : i + 1] for i in range(8)] for p in range(n)]
    parts_fine = gains([e[:4] for e in every])
    parts_coarse = gains([e[4:] for e in every])

    for y in range(2):
        kc = k[:, planes[y]]
        before = jnp.where(row == 0, coefs[gx, 10 + y : 11 + y], pltpu.roll(kc, 1, 0))
        after = jnp.where(row == width - 1, coefs[gx + 2, 8 + y : 9 + y], pltpu.roll(kc, width - 1, 0))
        txb[y] = face(WEIGHTS[0], kc, before)
        txa[y] = face(WEIGHTS[0], kc, after)
        tzb[y] = jnp.where(lane == 0, 0.0, face(WEIGHTS[2], kc, pltpu.roll(kc, 1, 1)))
        tza[y] = jnp.where(lane == depth - 1, 0.0, face(WEIGHTS[2], kc, pltpu.roll(kc, depth - 1, 1)))
    ty[1] = face(WEIGHTS[1], k[:, planes[0]], k[:, planes[1]])

    for way in range(2):
        wait_halo(0, way, src.at[:, ends_of[way]])
        multiply(halo[0, way], 2 + way)
    previous, after, sent0 = solve_ends(0, [0, 1, 2, 3], parts_fine)
    for y in range(2):
        u_s[0, y] = corrected(y, previous, after, 0)
    for way in range(2):
        u_h[way] = corrected(2 + way, previous, after, 0)
    sums = [previous[0:2], after[0:2]]
    all_sent = [first_gather, sent0]

    for way in range(2):
        wait_halo(1, way, k.at[:, ends_of[way]])
        ty[2 * way] = face(WEIGHTS[1], halo[1, way], k[:, planes[way]])

    def inner_residual(t, y):
        u = u_s[t, y]
        before = jnp.where(row == 0, sums[0][y : y + 1], pltpu.roll(u, 1, 0))
        after = jnp.where(row == width - 1, sums[1][y : y + 1], pltpu.roll(u, width - 1, 0))
        total = STORAGE * u + txb[y] * (u - before) + txa[y] * (u - after)
        total = total + ty[1] * (u - u_s[t, 1 - y])
        total = total + tzb[y] * (u - pltpu.roll(u, 1, 1)) + tza[y] * (u - pltpu.roll(u, depth - 1, 1))
        r_s[y] = src[:, planes[y]] - total

    def outer_residual(t, y, beside):
        return r_s[y] - ty[2 * y] * (u_s[t, y] - beside)

    for t in range(1, NSWEEP):
        for y in range(2):
            inner_residual(t - 1, y)
        for y in range(2):
            if t == 1:
                beside = u_h[y]
            else:
                wait_halo(t, y, u_s.at[t - 1, 1 - y])
                beside = halo[t, y]
            multiply(outer_residual(t - 1, y, beside), y)
        previous, after, more = solve_ends(t, [0, 1], parts_fine)
        all_sent.append(more)
        sums = [sums[0] + previous, sums[1] + after]
        for way in range(2):
            y = 1 - way
            u_s[t, y] = u_s[t - 1, y] + corrected(y, previous, after, 0)
            send_halo(t + 1, way, u_s.at[t, y])
    split_matrices(inv_c)
    for y in range(2):
        inner_residual(NSWEEP - 1, y)
        u_out[:, planes[y]] = u_s[NSWEEP - 1, y]
    coarse = None
    for y in range(2):
        wait_halo(NSWEEP, y, u_s.at[NSWEEP - 1, 1 - y])
        r = outer_residual(NSWEEP - 1, y, halo[NSWEEP, y])
        r_out[:, planes[y]] = r
        coarse = r if coarse is None else 0.5 * (coarse + r)
    multiply(coarse, 0)
    previous, after, more = solve_ends(NSWEEP, [0], parts_coarse)
    all_sent.append(more)
    sm[...] = corrected(0, previous, after, 2).reshape(sm.shape)

    def exchange(i, source, target):
        out = []
        for d in range(1, m):
            peer = lax.rem(gy + d, m)
            out.append(pltpu.make_async_remote_copy(
                src_ref=source.at[peer], dst_ref=target.at[gy],
                send_sem=a_send.at[i, d - 1], recv_sem=a_recv.at[i, d - 1],
                device_id={"gy": peer}, device_id_type=MESH))
        for c in out:
            c.start()
        target[gy] = source[gy]
        for c in out:
            c.wait_recv()
        return out

    all_sent.append(exchange(0, sm, got))

    def mix_rows(j, _):
        def add(i, total):
            return total + same[j, i] * got[i]
        mix[j] = lax.fori_loop(0, m, add, jnp.zeros(got.shape[1:], F32))
        return 0

    lax.fori_loop(0, m, mix_rows, 0)
    all_sent.append(exchange(1, mix, back))
    c_out[...] = back[...]
    for copies in all_sent:
        for c in copies:
            c.wait_send()
    for kind, ref in ((0, src), (1, k)):
        for way in range(2):
            sent_halo(kind, way, ref.at[:, ends_of[way]])
    for t in range(1, NSWEEP):
        for way in range(2):
            sent_halo(t + 1, way, u_s.at[t, 1 - way])


def local(source, perm, layer_ids, inv_fine, cpl_fine, inv_coarse, cpl_coarse, owner_map):
    width, planes, depth = source.shape
    n, m = lax.axis_size("gx"), lax.axis_size("gy")
    owners = owner_map[:, 0]
    same = (owners[:, None] == owners[None, :]).astype(F32)
    chunk = (m, width // m, depth)
    plane = (width, depth)
    flat = (width, planes * depth)
    vmem = pl.BlockSpec(memory_space=pltpu.VMEM)
    u, r, c = pl.pallas_call(
        functools.partial(kernel, n, m),
        out_shape=[jax.ShapeDtypeStruct(flat, F32), jax.ShapeDtypeStruct(flat, F32), jax.ShapeDtypeStruct(chunk, F32)],
        in_specs=[vmem] * 5 + [pl.BlockSpec(memory_space=pltpu.SMEM)] * 3,
        out_specs=[vmem] * 3,
        scratch_shapes=[
            pltpu.VMEM(inv_fine.shape, BF16),
            pltpu.VMEM(inv_fine.shape, BF16),
            pltpu.VMEM(plane, BF16),
            pltpu.VMEM(plane, BF16),
            pltpu.VMEM((4,) + plane, F32),
            pltpu.VMEM((4, 2) + plane, F32),
            pltpu.VMEM((NSWEEP, 2) + plane, F32),
            pltpu.VMEM((2,) + plane, F32),
            pltpu.VMEM((2,) + plane, F32),
            pltpu.VMEM((2,) + plane, F32),
            pltpu.VMEM((2,) + plane, F32),
            pltpu.VMEM((2,) + plane, F32),
            pltpu.VMEM((2,) + plane, F32),
            pltpu.VMEM((3,) + plane, F32),
            pltpu.VMEM((n + 2, 16, depth), F32),
            pltpu.VMEM((NSWEEP + 1, n + 2, 8, depth), F32),
            pltpu.VMEM(chunk, F32),
            pltpu.VMEM(chunk, F32),
            pltpu.VMEM(chunk, F32),
            pltpu.VMEM(chunk, F32),
            pltpu.VMEM((4,) + plane, F32),
            pltpu.SemaphoreType.DMA((4, 2)),
            pltpu.SemaphoreType.DMA((4, 2)),
            pltpu.SemaphoreType.DMA((NSWEEP + 2, n - 1)),
            pltpu.SemaphoreType.DMA((NSWEEP + 2, n - 1)),
            pltpu.SemaphoreType.DMA((2, m - 1)),
            pltpu.SemaphoreType.DMA((2, m - 1)),
        ],
        compiler_params=pltpu.CompilerParams(collective_id=0, has_side_effects=True, vmem_limit_bytes=56 << 20),
    )(source.reshape(flat), perm.reshape(flat), inv_fine, inv_coarse, layer_ids[None], cpl_fine, cpl_coarse, same)
    return u.reshape(source.shape), r.reshape(source.shape), c.reshape(width, 1, depth)


def solution(mesh):
    in_specs = (
        P("gx", "gy", None),
        P("gx", "gy", None),
        P(),
        P(None, "gx", None),
        P(None, None, "gx"),
        P(None, "gx", None),
        P(None, None, "gx"),
        P(),
    )
    out_specs = (P("gx", "gy", None), P("gx", "gy", None), P("gx", "gy", None))
    return jax.shard_map(local, mesh=mesh, in_specs=in_specs, out_specs=out_specs, check_vma=False)
```
